32 devices in a mesh: dp: 4 (over z), shard: 8 (over y, x, core).
Axes of the slice: x: 2, y: 2, z: 4, core: 2. Of those that a mesh axis runs over, the one named last changes fastest.
Arguments:
- grads: bfloat16 [4, 16, 256, 256], P('dp', None, 'shard'), may hold values from -24 to 24
- owner_table: int32 [4, 16], replicated, may hold values from 0 to 3, as said below
- block_counts: int32 [4, 8], replicated, may hold values from 0 to 2, as said below
- prev_left: float32 [64, 256, 256], P(('dp', 'shard')), as said below
- prev_right: float32 [64, 256, 256], P(('dp', 'shard')), as said below
Outputs:
- updates: bfloat16 [16, 256, 256], P(None, 'shard')
The draws below stay inside these ranges and needn't reach their ends.
Inputs may be any that keep to these rules, and one draw needn't show every extreme that they name: `owner_table`: for group d and owner o, entries o * 2 to o * 2 + block_counts[d, o] - 1 of row d name blocks of the group, and these live entries together name each of the group's 4 blocks exactly once; the other entries name arbitrary blocks of the group. `block_counts`: each row sums to 4; in every row some owner has exactly 2 blocks. `prev_left`: each slot's matrix is symmetric positive semidefinite. `prev_right`: each slot's matrix is symmetric positive semidefinite.
All inputs are finite; a program needn't handle non-finite values.
Results may differ from the reference program's by a relative error of at most 0.02.
Values may be sent and summed in bfloat16 or wider, within the bound.
A program may use at most 64 MiB of HBM per device.

```python
import jax
import jax.numpy as jnp
from jax import lax

BS = 256
CAP = 2
GROUPS = 4
OWNERS = 8
BPG = 4
NB = 16
SLOTS = 64


def assignment(key):
    base = jax.random.fold_in(key, 7)

    def one_group(group_key):
        key_rank, key_force, key_perm, key_fill = jax.random.split(group_key, 4)
        slot_total = OWNERS * CAP
        slot_ids = jnp.arange(slot_total, dtype=jnp.int32)
        ranking = jax.random.permutation(key_rank, slot_total).astype(jnp.int32)
        forced = jax.random.randint(key_force, (), 0, OWNERS, dtype=jnp.int32)
        priority = jnp.where(slot_ids // CAP == forced, ranking - slot_total, ranking)
        ordering = jnp.argsort(priority, stable=True)
        placed = jnp.argsort(ordering, stable=True)
        chosen = (placed < BPG).astype(jnp.int32)
        counts = jnp.sum(chosen.reshape(OWNERS, CAP), axis=1).astype(jnp.int32)
        is_live = slot_ids % CAP < counts[slot_ids // CAP]
        position = jnp.cumsum(is_live.astype(jnp.int32)) - 1
        shuffled = jax.random.permutation(key_perm, BPG).astype(jnp.int32)
        filler = jax.random.randint(key_fill, (slot_total,), 0, BPG, dtype=jnp.int32)
        owner_rows = jnp.where(is_live, shuffled[jnp.clip(position, 0, BPG - 1)], filler)
        return (owner_rows.astype(jnp.int32), counts)
    return jax.vmap(one_group)(jax.random.split(base, GROUPS))


def draw_owner_table(key, part):
    return assignment(key)[0]


def draw_block_counts(key, part):
    return assignment(key)[1]


def draw_grads(key, part):
    base = jax.random.fold_in(key, 17)
    key_noise = jax.random.fold_in(base, 0)
    key_rows = jax.random.fold_in(base, 1)
    key_cols = jax.random.fold_in(base, 2)
    key_left = jax.random.fold_in(base, 4)
    key_right = jax.random.fold_in(base, 5)
    row_scale = 10.0 ** jax.random.uniform(key_rows, (NB, BS, 1), jnp.float32, -0.5, 0.5)
    col_scale = 10.0 ** jax.random.uniform(key_cols, (NB, 1, BS), jnp.float32, -0.5, 0.5)
    left_vec = jax.random.normal(key_left, (NB, BS, 1), jnp.float32)
    right_vec = jax.random.normal(key_right, (NB, 1, BS), jnp.float32)
    paired = left_vec * right_vec
    noise = jax.random.normal(key_noise, (GROUPS, NB, BS, BS), jnp.float32)
    values = 0.25 * noise + 0.18 / jnp.sqrt(jnp.float32(GROUPS)) * paired[None]
    return jnp.clip(values * row_scale * col_scale, -24.0, 24.0).astype(jnp.bfloat16)


def statistic(key, salt):
    base = jax.random.fold_in(key, salt)
    key_entries, key_rows, key_common = jax.random.split(base, 3)
    decades = 28.0
    variance = GROUPS / 16.0
    entries = jax.random.normal(key_entries, (SLOTS, BS, BS), jnp.float32)
    shared = jax.random.normal(key_common, (SLOTS, 1, BS), jnp.float32)
    level_draw = jax.random.uniform(key_rows, (SLOTS, BS, 1), jnp.float32, 0.0, 1.0)
    row_scale = 10.0 ** (-0.5 * decades * level_draw)
    factor = (entries + 0.25 * shared) * row_scale
    gram_matrix = jnp.einsum('sik,sjk->sij', factor, factor, precision=lax.Precision.HIGHEST) / BS
    gram_matrix = 0.5 * (gram_matrix + jnp.swapaxes(gram_matrix, 1, 2))
    weight = 3.0 * variance * BS * jnp.sqrt(jnp.float32(BS))
    return weight * gram_matrix


def draw_prev_left(key, part):
    return statistic(key, 11)


def draw_prev_right(key, part):
    return statistic(key, 13)


def setup_inputs(seed: int = 0) -> dict:
    seeds = jax.random.split(jax.random.key(seed), 6)
    grads = draw_grads(jax.random.fold_in(seeds[5], 71), 0)
    owner_table = draw_owner_table(jax.random.fold_in(seeds[5], 71), 0)
    block_counts = draw_block_counts(jax.random.fold_in(seeds[5], 71), 0)
    prev_left = draw_prev_left(jax.random.fold_in(seeds[5], 71), 0)
    prev_right = draw_prev_right(jax.random.fold_in(seeds[5], 71), 0)
    return dict(grads=grads, owner_table=owner_table, block_counts=block_counts, prev_left=prev_left, prev_right=prev_right)


stat_decay = 0.9
eps_small = 1e-06

def inverse_root(factor):
    size_now = factor.shape[0]
    unit_matrix = jnp.eye(size_now, dtype=jnp.float32)
    norm_scale = size_now * jnp.sqrt(jnp.mean(factor * factor) + eps_small)
    start = factor / norm_scale
    first = (1.25 * unit_matrix - 0.25 * start).astype(jnp.bfloat16)
    square = jnp.dot(first, first, preferred_element_type=jnp.float32).astype(jnp.bfloat16)
    fourth = jnp.dot(square, square, preferred_element_type=jnp.float32).astype(jnp.bfloat16)
    next_state = jnp.dot(fourth, start.astype(jnp.bfloat16), preferred_element_type=jnp.float32)
    second = (1.25 * unit_matrix - 0.25 * next_state).astype(jnp.bfloat16)
    return jnp.dot(first, second, preferred_element_type=jnp.float32).astype(jnp.bfloat16)

def precondition(grad_block, left_prev, right_prev):
    left_factor = stat_decay * left_prev + (1.0 - stat_decay) * jnp.dot(grad_block, grad_block.T, preferred_element_type=jnp.float32)
    right_factor = stat_decay * right_prev + (1.0 - stat_decay) * jnp.dot(grad_block.T, grad_block, preferred_element_type=jnp.float32)
    root_left = inverse_root(left_factor)
    root_right = inverse_root(right_factor)
    half_done = jnp.dot(root_left, grad_block, preferred_element_type=jnp.float32).astype(jnp.bfloat16)
    precond = jnp.dot(half_done, root_right, preferred_element_type=jnp.float32)
    grad_wide = grad_block.astype(jnp.float32)
    grad_norm = jnp.sqrt(jnp.mean(grad_wide * grad_wide) + eps_small)
    cond_norm = jnp.sqrt(jnp.mean(precond * precond) + eps_small)
    return (precond * (grad_norm / cond_norm)).astype(jnp.bfloat16)

def reference(grads, owner_table, block_counts, prev_left, prev_right):

    def add_replica(running, replica):
        return (running + replica.astype(jnp.float32), None)
    total, unused = lax.scan(add_replica, jnp.zeros(grads.shape[1:], jnp.float32), grads)
    summed = total.astype(jnp.bfloat16)
    slot_total = OWNERS * CAP
    slot_ids = jnp.arange(slot_total, dtype=jnp.int32)
    is_live = (slot_ids % CAP)[None, :] < block_counts[:, slot_ids // CAP]
    matches = (owner_table[:, None, :] == jnp.arange(BPG, dtype=jnp.int32)[None, :, None]) & is_live[:, None, :]
    earliest = lax.optimization_barrier(jnp.min(jnp.where(matches, slot_ids[None, None, :], slot_total), axis=2))
    has_slot = (earliest < slot_total).reshape(-1)
    earliest = jnp.minimum(earliest, slot_total - 1)
    group_ids = jnp.arange(GROUPS, dtype=jnp.int32)[:, None]
    stat_index = ((group_ids * OWNERS + earliest // CAP) * CAP + earliest % CAP).reshape(-1).astype(jnp.int32)

    def one_block(inputs):
        grad_block, index_now, present = inputs
        update = precondition(grad_block, prev_left[index_now], prev_right[index_now])
        return jnp.where(present, update, jnp.zeros_like(update))
    return lax.map(one_block, (summed, stat_index, has_slot))
```

```python
import functools

import jax
import jax.numpy as jnp
from jax import lax
from jax.experimental import pallas as pl
from jax.experimental.pallas import tpu as pltpu
from jax.sharding import PartitionSpec as P

CAP = 2
MESH = pl.DeviceIdType.MESH


stat_decay = 0.9
eps_small = 1e-06


def inverse_root(factor):
    size_now = factor.shape[0]
    unit_matrix = jnp.eye(size_now, dtype=jnp.float32)
    norm_scale = size_now * jnp.sqrt(jnp.mean(factor * factor) + eps_small)
    start = factor / norm_scale
    first = (1.25 * unit_matrix - 0.25 * start).astype(jnp.bfloat16)
    square = jnp.dot(first, first, preferred_element_type=jnp.float32).astype(jnp.bfloat16)
    fourth = jnp.dot(square, square, preferred_element_type=jnp.float32).astype(jnp.bfloat16)
    next_state = jnp.dot(fourth, start.astype(jnp.bfloat16), preferred_element_type=jnp.float32)
    second = (1.25 * unit_matrix - 0.25 * next_state).astype(jnp.bfloat16)
    return jnp.dot(first, second, preferred_element_type=jnp.float32).astype(jnp.bfloat16)


def precondition(grad_block, left_prev, right_prev):
    left_factor = stat_decay * left_prev + (1.0 - stat_decay) * jnp.dot(
        grad_block, grad_block.T, preferred_element_type=jnp.float32
    )
    right_factor = stat_decay * right_prev + (1.0 - stat_decay) * jnp.dot(
        grad_block.T, grad_block, preferred_element_type=jnp.float32
    )
    root_left = inverse_root(left_factor)
    root_right = inverse_root(right_factor)
    half_done = jnp.dot(root_left, grad_block, preferred_element_type=jnp.float32).astype(
        jnp.bfloat16
    )
    precond = jnp.dot(half_done, root_right, preferred_element_type=jnp.float32)
    grad_wide = grad_block.astype(jnp.float32)
    grad_norm = jnp.sqrt(jnp.mean(grad_wide * grad_wide) + eps_small)
    cond_norm = jnp.sqrt(jnp.mean(precond * precond) + eps_small)
    return (precond * (grad_norm / cond_norm)).astype(jnp.bfloat16)


def refresh(arrived, prev_left, prev_right):
    return jax.vmap(precondition)(arrived, prev_left, prev_right)


def body(grads, owner_table, block_counts, prev_left, prev_right):
    owners = lax.axis_size("shard")
    groups = lax.axis_size("dp")
    my_group = lax.axis_index("dp")
    blocks = grads.shape[1]
    row_count = grads.shape[2]
    block_width = grads.shape[3]
    per_group = blocks // groups
    slot_total = owners * CAP
    slot_ids = jnp.arange(slot_total, dtype=jnp.int32)
    is_live = (slot_ids % CAP)[None, :] < block_counts[:, slot_ids // CAP]
    matches = (
        owner_table[:, None, :] == jnp.arange(per_group, dtype=jnp.int32)[None, :, None]
    ) & is_live[:, None, :]
    earliest = jnp.min(jnp.where(matches, slot_ids[None, None, :], slot_total), axis=2)
    has_slot = earliest < slot_total
    earliest = jnp.minimum(earliest, slot_total - 1)
    pick_index = earliest % CAP * owners + earliest // CAP
    local_terms = grads[0].astype(jnp.float32)
    summed = lax.psum_scatter(
        local_terms.astype(jnp.bfloat16), "dp", scatter_dimension=0, tiled=True
    )
    table_row = owner_table[my_group].reshape(owners, CAP).T
    outgoing = jnp.take(summed, table_row, axis=0)
    arrived = lax.all_to_all(outgoing, "shard", split_axis=1, concat_axis=1, tiled=True).reshape(
        CAP, block_width, block_width
    )
    fresh = refresh(arrived, prev_left, prev_right)
    returned = lax.all_to_all(
        fresh.reshape(CAP, owners, row_count, block_width),
        "shard",
        split_axis=1,
        concat_axis=1,
        tiled=True,
    )
    chosen = jnp.take(
        returned.reshape(CAP * owners, row_count, block_width), pick_index[my_group], axis=0
    )
    chosen = jnp.where(has_slot[my_group][:, None, None], chosen, jnp.zeros_like(chosen))
    return lax.all_gather(chosen, "dp", axis=0, tiled=True)


def start_factor(factor, unit_matrix):
    size_now = factor.shape[0]
    mean_square = jnp.sum(factor * factor, keepdims=True) * (1.0 / (size_now * size_now))
    inverse_scale = 1.0 / (size_now * jnp.sqrt(mean_square + eps_small))
    start = factor * inverse_scale
    first = (1.25 * unit_matrix - 0.25 * start).astype(jnp.bfloat16)
    return start.astype(jnp.bfloat16), first


def dot(a, b):
    return jnp.dot(a, b, preferred_element_type=jnp.float32)


def refresh_slot(grad_block, left_prev, right_prev):
    size_now = grad_block.shape[0]
    rows = lax.broadcasted_iota(jnp.int32, (size_now, size_now), 0)
    cols = lax.broadcasted_iota(jnp.int32, (size_now, size_now), 1)
    unit_matrix = jnp.where(rows == cols, 1.0, 0.0).astype(jnp.float32)
    gram_left = lax.dot_general(
        grad_block, grad_block, (((1,), (1,)), ((), ())), preferred_element_type=jnp.float32
    )
    gram_right = lax.dot_general(
        grad_block, grad_block, (((0,), (0,)), ((), ())), preferred_element_type=jnp.float32
    )
    factors = (
        stat_decay * left_prev + (1.0 - stat_decay) * gram_left,
        stat_decay * right_prev + (1.0 - stat_decay) * gram_right,
    )
    pairs = [start_factor(factor, unit_matrix) for factor in factors]
    squares = [dot(first, first).astype(jnp.bfloat16) for _, first in pairs]
    fourths = [dot(square, square).astype(jnp.bfloat16) for square in squares]
    states = [dot(fourth, start) for fourth, (start, _) in zip(fourths, pairs)]
    seconds = [(1.25 * unit_matrix - 0.25 * state).astype(jnp.bfloat16) for state in states]
    roots = [
        dot(first, second).astype(jnp.bfloat16) for (_, first), second in zip(pairs, seconds)
    ]
    half_done = dot(roots[0], grad_block).astype(jnp.bfloat16)
    precond = dot(half_done, roots[1])
    grad_wide = grad_block.astype(jnp.float32)
    share = 1.0 / (size_now * size_now)
    grad_norm = jnp.sqrt(jnp.sum(grad_wide * grad_wide, keepdims=True) * share + eps_small)
    cond_norm = jnp.sqrt(jnp.sum(precond * precond, keepdims=True) * share + eps_small)
    return (precond * (grad_norm / cond_norm)).astype(jnp.bfloat16)


def kernel(
    groups,
    owners,
    table_ref,
    counts_ref,
    grads_ref,
    left_ref,
    right_ref,
    out_ref,
    own_terms,
    terms,
    summed,
    outgoing,
    arrived,
    left_held,
    right_held,
    fresh,
    returned,
    chosen,
    local_sems,
    sum_send,
    sum_recv,
    go_send,
    go_recv,
    back_send,
    back_recv,
    last_send,
    last_recv,
):
    my_group = lax.axis_index("dp")
    me = lax.axis_index("shard")
    per_group, row_count, _ = own_terms.shape
    slot_total = owners * CAP

    def group_at(step):
        return lax.rem(my_group + step, groups)

    def owner_at(step):
        return lax.rem(me + step, owners)

    def group_blocks(group):
        return pl.ds(group * per_group, per_group)

    def rows_of(owner):
        return pl.ds(pl.multiple_of(owner * row_count, row_count), row_count)

    own_copy = pltpu.make_async_copy(
        grads_ref.at[0, group_blocks(my_group)], own_terms, local_sems.at[0]
    )
    own_copy.start()
    held_copies = []
    for slot in range(CAP):
        for side, (source, held) in enumerate(((left_ref, left_held), (right_ref, right_held))):
            copy = pltpu.make_async_copy(
                source.at[slot], held.at[slot], local_sems.at[2 + slot * 2 + side]
            )
            copy.start()
            held_copies.append(copy)

    barrier = pltpu.get_barrier_semaphore()
    for step in range(1, groups):
        pl.semaphore_signal(
            barrier, inc=1, device_id=(group_at(step), me), device_id_type=MESH
        )
    for step in range(1, owners):
        pl.semaphore_signal(
            barrier, inc=1, device_id=(my_group, owner_at(step)), device_id_type=MESH
        )
    pl.semaphore_wait(barrier, groups + owners - 2)

    sum_copies = []
    for step in range(1, groups):
        copy = pltpu.make_async_remote_copy(
            src_ref=grads_ref.at[0, group_blocks(group_at(step))],
            dst_ref=terms.at[step - 1],
            send_sem=sum_send.at[step - 1],
            recv_sem=sum_recv.at[step - 1],
            device_id=(group_at(step), me),
            device_id_type=MESH,
        )
        copy.start()
        sum_copies.append(copy)

    picks = [jnp.int32(slot_total)] * per_group
    for slot in reversed(range(slot_total)):
        live = slot % CAP < counts_ref[my_group, slot // CAP]
        named = jnp.where(live, table_ref[my_group, slot], -1)
        picks = [jnp.where(named == block, slot, pick) for block, pick in enumerate(picks)]

    own_copy.wait()
    for copy in sum_copies:
        copy.wait_recv()
    total = own_terms[...].astype(jnp.float32)
    for step in range(groups - 1):
        total += terms[step].astype(jnp.float32)
    summed[...] = total.astype(jnp.bfloat16)

    go_copies = []
    for slot in range(CAP):
        slot_copies = []
        for step in range(1, owners):
            owner = owner_at(step)
            place = slot * owners + step
            outgoing[place] = summed[table_ref[my_group, owner * CAP + slot]]
            copy = pltpu.make_async_remote_copy(
                src_ref=outgoing.at[place],
                dst_ref=arrived.at[slot, rows_of(me)],
                send_sem=go_send.at[place],
                recv_sem=go_recv.at[place],
                device_id=(my_group, owner),
                device_id_type=MESH,
            )
            copy.start()
            slot_copies.append(copy)
        arrived[slot, rows_of(me)] = summed[table_ref[my_group, me * CAP + slot]]
        go_copies.append(slot_copies)

    back_copies = []
    for slot in range(CAP):
        for copy in held_copies[2 * slot : 2 * slot + 2] :
            copy.wait()
        for copy in go_copies[slot]:
            copy.wait_recv()
        fresh[slot] = refresh_slot(arrived[slot], left_held[slot], right_held[slot])
        for step in range(1, owners):
            owner = owner_at(step)
            place = slot * owners + step
            copy = pltpu.make_async_remote_copy(
                src_ref=fresh.at[slot, rows_of(owner)],
                dst_ref=returned.at[me * CAP + slot],
                send_sem=back_send.at[place],
                recv_sem=back_recv.at[place],
                device_id=(my_group, owner),
                device_id_type=MESH,
            )
            copy.start()
            back_copies.append(copy)
        returned[me * CAP + slot] = fresh[slot, rows_of(me)]

    for copy in back_copies:
        copy.wait_recv()
    for block, pick in enumerate(picks):
        keep = jnp.where(pick < slot_total, 1.0, 0.0).astype(jnp.float32)
        picked = returned[jnp.minimum(pick, slot_total - 1)]
        chosen[block] = (picked.astype(jnp.float32) * keep).astype(jnp.bfloat16)

    last_copies = []
    for step in range(1, groups):
        copy = pltpu.make_async_remote_copy(
            src_ref=chosen,
            dst_ref=out_ref.at[group_blocks(my_group)],
            send_sem=last_send.at[step - 1],
            recv_sem=last_recv.at[step - 1],
            device_id=(group_at(step), me),
            device_id_type=MESH,
        )
        copy.start()
        last_copies.append(copy)
    out_copy = pltpu.make_async_copy(
        chosen, out_ref.at[group_blocks(my_group)], local_sems.at[1]
    )
    out_copy.start()
    for copy in sum_copies + go_copies[0] + go_copies[1] + back_copies:
        copy.wait_send()
    out_copy.wait()
    for copy in last_copies:
        copy.wait()


def fused_body(grads, owner_table, block_counts, prev_left, prev_right):
    owners = lax.axis_size("shard")
    groups = lax.axis_size("dp")
    _, blocks, row_count, width = grads.shape
    per_group = blocks // groups
    dma = pltpu.SemaphoreType.DMA
    part = (per_group, row_count, width)
    return pl.pallas_call(
        functools.partial(kernel, groups, owners),
        out_shape=jax.ShapeDtypeStruct((blocks, row_count, width), jnp.bfloat16),
        in_specs=[pl.BlockSpec(memory_space=pltpu.SMEM)] * 2
        + [pl.BlockSpec(memory_space=pl.ANY)] * 3,
        out_specs=pl.BlockSpec(memory_space=pl.ANY),
        scratch_shapes=[
            pltpu.VMEM(part, jnp.bfloat16),
            pltpu.VMEM((groups - 1,) + part, jnp.bfloat16),
            pltpu.VMEM(part, jnp.bfloat16),
            pltpu.VMEM((CAP * owners, row_count, width), jnp.bfloat16),
            pltpu.VMEM((CAP, width, width), jnp.bfloat16),
            pltpu.VMEM((CAP, width, width), jnp.float32),
            pltpu.VMEM((CAP, width, width), jnp.float32),
            pltpu.VMEM((CAP, width, width), jnp.bfloat16),
            pltpu.VMEM((CAP * owners, row_count, width), jnp.bfloat16),
            pltpu.VMEM(part, jnp.bfloat16),
            dma((2 + 2 * CAP,)),
            dma((groups - 1,)),
            dma((groups - 1,)),
            dma((CAP * owners,)),
            dma((CAP * owners,)),
            dma((CAP * owners,)),
            dma((CAP * owners,)),
            dma((groups - 1,)),
            dma((groups - 1,)),
        ],
        compiler_params=pltpu.CompilerParams(
            collective_id=0, has_side_effects=True, vmem_limit_bytes=48 * 1024 * 1024
        ),
    )(owner_table, block_counts, grads, prev_left, prev_right)


def either_body(grads, *others):
    if grads.shape[2] % 16:
        return body(grads, *others)
    return fused_body(grads, *others)


def solution(mesh):
    return jax.shard_map(
        either_body,
        mesh=mesh,
        in_specs=(
            P("dp", None, "shard", None),
            P(),
            P(),
            P(("dp", "shard"), None, None),
            P(("dp", "shard"), None, None),
        ),
        out_specs=P(None, "shard", None),
        check_vma=False,
    )
```

```python
import functools

import jax
import jax.numpy as jnp
from jax import lax
from jax.experimental import pallas as pl
from jax.experimental.pallas import tpu as pltpu
from jax.sharding import PartitionSpec as P

CAP = 2
MESH = pl.DeviceIdType.MESH


stat_decay = 0.9
eps_small = 1e-06


def inverse_root(factor):
    size_now = factor.shape[0]
    unit_matrix = jnp.eye(size_now, dtype=jnp.float32)
    norm_scale = size_now * jnp.sqrt(jnp.mean(factor * factor) + eps_small)
    start = factor / norm_scale
    first = (1.25 * unit_matrix - 0.25 * start).astype(jnp.bfloat16)
    square = jnp.dot(first, first, preferred_element_type=jnp.float32).astype(jnp.bfloat16)
    fourth = jnp.dot(square, square, preferred_element_type=jnp.float32).astype(jnp.bfloat16)
    next_state = jnp.dot(fourth, start.astype(jnp.bfloat16), preferred_element_type=jnp.float32)
    second = (1.25 * unit_matrix - 0.25 * next_state).astype(jnp.bfloat16)
    return jnp.dot(first, second, preferred_element_type=jnp.float32).astype(jnp.bfloat16)


def precondition(grad_block, left_prev, right_prev):
    left_factor = stat_decay * left_prev + (1.0 - stat_decay) * jnp.dot(
        grad_block, grad_block.T, preferred_element_type=jnp.float32
    )
    right_factor = stat_decay * right_prev + (1.0 - stat_decay) * jnp.dot(
        grad_block.T, grad_block, preferred_element_type=jnp.float32
    )
    root_left = inverse_root(left_factor)
    root_right = inverse_root(right_factor)
    half_done = jnp.dot(root_left, grad_block, preferred_element_type=jnp.float32).astype(
        jnp.bfloat16
    )
    precond = jnp.dot(half_done, root_right, preferred_element_type=jnp.float32)
    grad_wide = grad_block.astype(jnp.float32)
    grad_norm = jnp.sqrt(jnp.mean(grad_wide * grad_wide) + eps_small)
    cond_norm = jnp.sqrt(jnp.mean(precond * precond) + eps_small)
    return (precond * (grad_norm / cond_norm)).astype(jnp.bfloat16)


def refresh(arrived, prev_left, prev_right):
    return jax.vmap(precondition)(arrived, prev_left, prev_right)


def body(grads, owner_table, block_counts, prev_left, prev_right):
    owners = lax.axis_size("shard")
    groups = lax.axis_size("dp")
    my_group = lax.axis_index("dp")
    blocks = grads.shape[1]
    row_count = grads.shape[2]
    block_width = grads.shape[3]
    per_group = blocks // groups
    slot_total = owners * CAP
    slot_ids = jnp.arange(slot_total, dtype=jnp.int32)
    is_live = (slot_ids % CAP)[None, :] < block_counts[:, slot_ids // CAP]
    matches = (
        owner_table[:, None, :] == jnp.arange(per_group, dtype=jnp.int32)[None, :, None]
    ) & is_live[:, None, :]
    earliest = jnp.min(jnp.where(matches, slot_ids[None, None, :], slot_total), axis=2)
    has_slot = earliest < slot_total
    earliest = jnp.minimum(earliest, slot_total - 1)
    pick_index = earliest % CAP * owners + earliest // CAP
    local_terms = grads[0].astype(jnp.float32)
    summed = lax.psum_scatter(
        local_terms.astype(jnp.bfloat16), "dp", scatter_dimension=0, tiled=True
    )
    table_row = owner_table[my_group].reshape(owners, CAP).T
    outgoing = jnp.take(summed, table_row, axis=0)
    arrived = lax.all_to_all(outgoing, "shard", split_axis=1, concat_axis=1, tiled=True).reshape(
        CAP, block_width, block_width
    )
    fresh = refresh(arrived, prev_left, prev_right)
    returned = lax.all_to_all(
        fresh.reshape(CAP, owners, row_count, block_width),
        "shard",
        split_axis=1,
        concat_axis=1,
        tiled=True,
    )
    chosen = jnp.take(
        returned.reshape(CAP * owners, row_count, block_width), pick_index[my_group], axis=0
    )
    chosen = jnp.where(has_slot[my_group][:, None, None], chosen, jnp.zeros_like(chosen))
    return lax.all_gather(chosen, "dp", axis=0, tiled=True)


def start_factor(factor, unit_matrix):
    size_now = factor.shape[0]
    mean_square = jnp.sum(factor * factor, keepdims=True) * (1.0 / (size_now * size_now))
    inverse_scale = 1.0 / (size_now * jnp.sqrt(mean_square + eps_small))
    start = factor * inverse_scale
    first = (1.25 * unit_matrix - 0.25 * start).astype(jnp.bfloat16)
    return start.astype(jnp.bfloat16), first


def dot(a, b):
    return jnp.dot(a, b, preferred_element_type=jnp.float32)


def refresh_slot(grad_block, left_prev, right_prev):
    size_now = grad_block.shape[0]
    rows = lax.broadcasted_iota(jnp.int32, (size_now, size_now), 0)
    cols = lax.broadcasted_iota(jnp.int32, (size_now, size_now), 1)
    unit_matrix = jnp.where(rows == cols, 1.0, 0.0).astype(jnp.float32)
    gram_left = lax.dot_general(
        grad_block, grad_block, (((1,), (1,)), ((), ())), preferred_element_type=jnp.float32
    )
    gram_right = lax.dot_general(
        grad_block, grad_block, (((0,), (0,)), ((), ())), preferred_element_type=jnp.float32
    )
    factors = (
        stat_decay * left_prev + (1.0 - stat_decay) * gram_left,
        stat_decay * right_prev + (1.0 - stat_decay) * gram_right,
    )
    pairs = [start_factor(factor, unit_matrix) for factor in factors]
    squares = [dot(first, first).astype(jnp.bfloat16) for _, first in pairs]
    products = [dot(first, start).astype(jnp.bfloat16) for start, first in pairs]
    fourths = [dot(square, square).astype(jnp.bfloat16) for square in squares]
    roots = [
        (1.25 * first.astype(jnp.float32) - 0.25 * dot(fourth, product)).astype(jnp.bfloat16)
        for fourth, product, (_, first) in zip(fourths, products, pairs)
    ]
    half_done = dot(roots[0], grad_block).astype(jnp.bfloat16)
    precond = dot(half_done, roots[1])
    grad_wide = grad_block.astype(jnp.float32)
    share = 1.0 / (size_now * size_now)
    grad_norm = jnp.sqrt(jnp.sum(grad_wide * grad_wide, keepdims=True) * share + eps_small)
    cond_norm = jnp.sqrt(jnp.sum(precond * precond, keepdims=True) * share + eps_small)
    return (precond * (grad_norm / cond_norm)).astype(jnp.bfloat16)


def rank_slots(group, step, groups, owners, table_ref, counts_ref, ranks):
    per_group = ranks.shape[0] // groups
    found = jnp.int32(0)
    places = [jnp.int32(0)] * per_group
    block_ranks = [jnp.int32(-1)] * per_group
    for place in range(CAP * owners):
        slot, owner = place // owners, place % owners
        live = slot < counts_ref[group, owner]
        named = jnp.where(live, table_ref[group, owner * CAP + slot], -1)
        block_ranks = [
            jnp.where(named == block, found, rank) for block, rank in enumerate(block_ranks)
        ]
        if step == 0:
            open_rank = jnp.where(live, found, -1)
            places = [
                jnp.where(open_rank == rank, place, held) for rank, held in enumerate(places)
            ]
        found = found + live.astype(jnp.int32)
    for block, rank in enumerate(block_ranks):
        ranks[step * per_group + block] = rank
    return places


def kernel(
    groups,
    owners,
    table_hbm,
    counts_hbm,
    grads_ref,
    left_ref,
    right_ref,
    out_ref,
    table_ref,
    counts_ref,
    ranks,
    own_terms,
    terms,
    summed,
    outgoing,
    arrived,
    left_held,
    right_held,
    fresh,
    returned,
    returned_late,
    gathered,
    local_sems,
    sum_send,
    sum_recv,
    go_send,
    go_recv,
    back_send,
    back_recv,
    last_send,
    last_recv,
):
    my_group = lax.axis_index("dp")
    me = lax.axis_index("shard")
    per_group, row_count, _ = own_terms.shape
    slot_total = owners * CAP

    def group_at(step):
        return lax.rem(my_group + step, groups)

    def owner_at(step):
        return lax.rem(me + step, owners)

    def group_blocks(group):
        return pl.ds(group * per_group, per_group)

    def rows_of(owner):
        return pl.ds(pl.multiple_of(owner * row_count, row_count), row_count)

    table_copy = pltpu.make_async_copy(table_hbm, table_ref, local_sems.at[1])
    counts_copy = pltpu.make_async_copy(counts_hbm, counts_ref, local_sems.at[2])
    table_copy.start()
    counts_copy.start()
    own_copy = pltpu.make_async_copy(
        grads_ref.at[0, group_blocks(my_group)], own_terms, local_sems.at[0]
    )
    own_copy.start()
    held_copies = []
    for slot in range(CAP):
        for side, (source, held) in enumerate(((left_ref, left_held), (right_ref, right_held))):
            copy = pltpu.make_async_copy(
                source.at[slot], held.at[slot], local_sems.at[3 + slot * 2 + side]
            )
            copy.start()
            held_copies.append(copy)

    barrier = pltpu.get_barrier_semaphore()
    for step in range(1, groups):
        pl.semaphore_signal(
            barrier, inc=1, device_id=(group_at(step), me), device_id_type=MESH
        )
    for step in range(1, owners):
        pl.semaphore_signal(
            barrier, inc=1, device_id=(my_group, owner_at(step)), device_id_type=MESH
        )
    pl.semaphore_wait(barrier, groups + owners - 2)

    sum_copies = []
    for step in range(1, groups):
        copy = pltpu.make_async_remote_copy(
            src_ref=grads_ref.at[0, group_blocks(group_at(step))],
            dst_ref=terms.at[step - 1],
            send_sem=sum_send.at[step - 1],
            recv_sem=sum_recv.at[step - 1],
            device_id=(group_at(step), me),
            device_id_type=MESH,
        )
        copy.start()
        sum_copies.append(copy)

    table_copy.wait()
    counts_copy.wait()
    places = rank_slots(group_at(0), 0, groups, owners, table_ref, counts_ref, ranks)
    for step in range(1, groups):
        rank_slots(group_at(groups - step), step, groups, owners, table_ref, counts_ref, ranks)

    own_copy.wait()
    for copy in sum_copies:
        copy.wait_recv()
    total = own_terms[...].astype(jnp.float32)
    for step in range(groups - 1):
        total += terms[step].astype(jnp.float32)
    summed[...] = total.astype(jnp.bfloat16)

    go_copies = []
    for slot in range(CAP):
        slot_copies = []
        for step in range(1, owners):
            owner = owner_at(step)
            place = slot * owners + step
            outgoing[place] = summed[table_ref[my_group, owner * CAP + slot]]
            copy = pltpu.make_async_remote_copy(
                src_ref=outgoing.at[place],
                dst_ref=arrived.at[slot, rows_of(me)],
                send_sem=go_send.at[place],
                recv_sem=go_recv.at[place],
                device_id=(my_group, owner),
                device_id_type=MESH,
            )
            copy.start()
            slot_copies.append(copy)
        arrived[slot, rows_of(me)] = summed[table_ref[my_group, me * CAP + slot]]
        go_copies.append(slot_copies)

    early = -(-per_group // CAP)
    parts = (range(early), range(early, per_group))
    landing = (returned, returned_late)
    back_copies = []
    last_copies = []
    for slot in range(CAP):
        for copy in held_copies[2 * slot : 2 * slot + 2]:
            copy.wait()
        for copy in go_copies[slot]:
            copy.wait_recv()
        fresh[slot] = refresh_slot(arrived[slot], left_held[slot], right_held[slot])
        slot_copies = []
        for step in range(1, owners):
            owner = owner_at(step)
            place = slot * owners + step
            copy = pltpu.make_async_remote_copy(
                src_ref=fresh.at[slot, rows_of(owner)],
                dst_ref=landing[slot].at[me],
                send_sem=back_send.at[place],
                recv_sem=back_recv.at[place],
                device_id=(my_group, owner),
                device_id_type=MESH,
            )
            copy.start()
            slot_copies.append(copy)
        landing[slot][me] = fresh[slot, rows_of(me)]
        back_copies.append(slot_copies)

    for slot in range(CAP):
        for copy in back_copies[slot]:
            copy.wait_recv()
        for rank in parts[slot]:
            picked = returned[jnp.minimum(places[rank], owners - 1)]
            if slot:
                late = returned_late[jnp.maximum(places[rank] - owners, 0)]
                picked = lax.select(places[rank] < owners, picked, late)
            gathered[0, rank] = picked
        piece = pl.ds(parts[slot].start, len(parts[slot]))
        for step in range(1, groups):
            copy = pltpu.make_async_remote_copy(
                src_ref=gathered.at[0, piece],
                dst_ref=gathered.at[step, piece],
                send_sem=last_send.at[slot * groups + step],
                recv_sem=last_recv.at[slot * groups + step],
                device_id=(group_at(step), me),
                device_id_type=MESH,
            )
            copy.start()
            last_copies.append(copy)
    for copy in sum_copies + sum(go_copies, []) + sum(back_copies, []):
        copy.wait_send()
    for copy in last_copies:
        copy.wait_recv()
    for step in range(groups):
        group = group_at(groups - step)
        for block in range(per_group):
            rank = ranks[step * per_group + block]
            keep = jnp.where(rank >= 0, 1.0, 0.0).astype(jnp.float32)
            picked = gathered[step, jnp.maximum(rank, 0)].astype(jnp.float32)
            out_ref[group * per_group + block] = (picked * keep).astype(jnp.bfloat16)
    for copy in last_copies:
        copy.wait_send()


def fused_body(grads, owner_table, block_counts, prev_left, prev_right):
    owners = lax.axis_size("shard")
    groups = lax.axis_size("dp")
    _, blocks, row_count, width = grads.shape
    per_group = blocks // groups
    dma = pltpu.SemaphoreType.DMA
    part = (per_group, row_count, width)
    return pl.pallas_call(
        functools.partial(kernel, groups, owners),
        out_shape=jax.ShapeDtypeStruct((blocks, row_count, width), jnp.bfloat16),
        in_specs=[pl.BlockSpec(memory_space=pltpu.HBM)] * 5,
        out_specs=pl.BlockSpec(memory_space=pltpu.VMEM),
        scratch_shapes=[
            pltpu.SMEM(owner_table.shape, jnp.int32),
            pltpu.SMEM(block_counts.shape, jnp.int32),
            pltpu.SMEM((blocks,), jnp.int32),
            pltpu.VMEM(part, jnp.bfloat16),
            pltpu.VMEM((groups - 1,) + part, jnp.bfloat16),
            pltpu.VMEM(part, jnp.bfloat16),
            pltpu.VMEM((CAP * owners, row_count, width), jnp.bfloat16),
            pltpu.VMEM((CAP, width, width), jnp.bfloat16),
            pltpu.VMEM((CAP, width, width), jnp.float32),
            pltpu.VMEM((CAP, width, width), jnp.float32),
            pltpu.VMEM((CAP, width, width), jnp.bfloat16),
            pltpu.VMEM((owners, row_count, width), jnp.bfloat16),
            pltpu.VMEM((owners, row_count, width), jnp.bfloat16),
            pltpu.VMEM((groups,) + part, jnp.bfloat16),
            dma((3 + 2 * CAP,)),
            dma((groups - 1,)),
            dma((groups - 1,)),
            dma((CAP * owners,)),
            dma((CAP * owners,)),
            dma((CAP * owners,)),
            dma((CAP * owners,)),
            dma((CAP * groups,)),
            dma((CAP * groups,)),
        ],
        compiler_params=pltpu.CompilerParams(
            collective_id=0, has_side_effects=True, vmem_limit_bytes=62 * 1024 * 1024
        ),
    )(owner_table, block_counts, grads, prev_left, prev_right)


def either_body(grads, *others):
    if grads.shape[2] % 16:
        return body(grads, *others)
    return fused_body(grads, *others)


def solution(mesh):
    return jax.shard_map(
        either_body,
        mesh=mesh,
        in_specs=(
            P("dp", None, "shard", None),
            P(),
            P(),
            P(("dp", "shard"), None, None),
            P(("dp", "shard"), None, None),
        ),
        out_specs=P(None, "shard", None),
        check_vma=False,
    )
```
